768 devices in a mesh: row: 96 (over z, x, core), col: 8 (over y).
Axes of the slice: x: 4, y: 8, z: 12, core: 2. Of those that a mesh axis runs over, the one named last changes fastest.
Arguments:
- amplitudes: bfloat16 [96, 16, 393216], P(None, 'col', 'row'), may hold values from -20 to 20
- integrals: bfloat16 [3072, 8, 128, 128], P('row'), may hold values from -0.0390625 to 0.0390625
- tile_cols: int32 [3072, 8], P('row'), may hold values from -1 to 15, as said below
- pair_energy: float32 [96, 16], P('row'), may hold values from -2.5 to -1
- col_energy: float32 [2048], P('col'), may hold values from 0.2 to 1.5
Outputs:
- updated: bfloat16 [96, 16, 2048], P('row', None, 'col')
The draws below stay inside these ranges and needn't reach their ends.
Inputs may be any that keep to these rules, and one draw needn't show every extreme that they name: `tile_cols`: in each row the live entries come first and name distinct column tiles; the remaining entries are -1. Every cd tile has at least one live entry, and among the 32 cd tiles of each index of row one has all 8 entries live.
All inputs are finite; a program needn't handle non-finite values.
Results may differ from the reference program's by a relative error of at most 0.0024.
Values sent between devices are 32-bit elements; how exact they have to be, the bound alone decides.
No kernel may reach another device: no remote copies, remote signals or barrier semaphores. Data moves between devices by JAX's collectives and lax.ppermute only.
A program may use at most 64 MiB of HBM per device.

```python
import jax
import jax.numpy as jnp
from jax import lax

TILE = 128
KR = 32
NS = 8
NJ = 16
NK = 3072
PC = 16
N_ROW = 96


def draw_tile_cols(key, part):
    key = jax.random.fold_in(key, 11)
    key_perm, key_live, key_full = jax.random.split(key, 3)
    orders = jax.vmap(lambda sub: jax.random.permutation(sub, NJ))(jax.random.split(key_perm, NK))[:, :NS]
    live = jax.random.randint(key_live, (NK,), 1, NS + 1)
    chosen = jax.random.randint(key_full, (NK // KR,), 0, KR)
    position = jnp.arange(NK, dtype=jnp.int32)
    full_mask = position % KR == chosen[position // KR]
    live = jnp.where(full_mask, NS, live)
    slot_ids = jnp.arange(NS, dtype=jnp.int32)
    return jnp.where(slot_ids[None, :] < live[:, None], orders, -1).astype(jnp.int32)


def with_spikes(values, own_key, source, target, blocks, factor):
    owner, partner = [(jnp.arange(values.shape[dim]) // (values.shape[dim] // blocks)).reshape([-1 if axis == dim else 1 for axis in range(values.ndim)]) for dim in (source, target)]
    chosen = jax.random.permutation(own_key, blocks)[partner]
    strong = (owner == chosen) | (owner == (partner + blocks // 2) % blocks)
    return jnp.where(strong, factor * values, values)


def levels(stream_key, extent, cuts, low, largest):
    factor_of = 1.0
    for axis_at, parts in cuts:
        steps = jax.random.uniform(jax.random.fold_in(jax.random.fold_in(stream_key, 6), axis_at), (parts,), jnp.float32, low / len(cuts), largest / len(cuts))
        factor_of = factor_of * jnp.repeat(jnp.exp(steps), extent[axis_at] // parts).reshape((-1,) + (1,) * (len(extent) - 1 - axis_at))
    return factor_of


def scatter_about(rng, dims, width, reach, shards=(), kind=jnp.bfloat16):
    gain = levels(rng, dims, shards, -0.22, 0.18) if shards else 1.0
    result = jax.random.normal(rng, dims, jnp.float32) * width * gain
    return jnp.minimum(jnp.maximum(result, -reach), reach).astype(kind)


def bell_draw_with(key, extent, scale, reach, cuts, heavy, held_as=jnp.bfloat16):
    result = scale * jax.random.normal(key, extent, jnp.float32)
    if cuts:
        result = result * levels(key, extent, cuts, -0.22, 0.18)
    return jnp.clip(with_spikes(result, jax.random.fold_in(key, 3), *heavy), -reach, reach).astype(held_as)


def setup_inputs(seed: int = 0) -> dict:
    key_list = jax.random.split(jax.random.key(seed), 6)
    amplitudes = bell_draw_with(key_list[0], (N_ROW, PC, NK * TILE), 1.0, 20.0, ((1, 8), (2, 96)), (2, 0, 96, 4.75))
    integrals = scatter_about(key_list[1], (NK, NS, TILE, TILE), (NK * (NS + 1) * TILE // (8 * NJ)) ** -0.5, 0.0390625, ((0, 96),))
    tile_cols = draw_tile_cols(jax.random.fold_in(key_list[5], 71), 0)
    pair_energy = jnp.clip(-2.5 + 1.5 * jax.random.uniform(key_list[3], (N_ROW, PC), jnp.float32) ** levels(key_list[3], (N_ROW, PC), ((0, 96),), -0.2, 0.2), -2.5, -1.0)
    col_energy = jnp.clip(0.2 + 1.3 * jax.random.uniform(key_list[4], (NJ * TILE,), jnp.float32) ** levels(key_list[4], (NJ * TILE,), ((0, 8),), -0.2, 0.2), 0.2, 1.5)
    return {"amplitudes": amplitudes, "integrals": integrals, "tile_cols": tile_cols, "pair_energy": pair_energy, "col_energy": col_energy}


def reference(amplitudes, integrals, tile_cols, pair_energy, col_energy):
    rows = amplitudes.reshape(-1, NK, TILE)
    count = rows.shape[0]
    groups = NK // 8
    selector = (tile_cols[:, :, None] == jnp.arange(NJ, dtype=jnp.int32)[None, None, :]).astype(jnp.float32)
    left_all = rows.reshape(count, groups, 8, TILE).transpose(1, 0, 2, 3)
    right_all = integrals.reshape(groups, 8, NS, TILE, TILE)
    pick_all = selector.reshape(groups, 8, NS, NJ)

    def step(acc, inputs):
        left, right, pick = inputs
        prod = jnp.einsum('pkc,ksce->pkse', left.astype(jnp.float32), right.astype(jnp.float32), precision=lax.Precision.HIGHEST)
        return acc + jnp.einsum('pkse,ksj->pje', prod, pick, precision=lax.Precision.HIGHEST), None

    start = jnp.zeros((count, NJ, TILE), jnp.float32)
    ladder, _ = lax.scan(step, start, (left_all, right_all, pick_all))
    ladder = ladder.reshape(N_ROW, PC, NJ * TILE)
    denom = pair_energy[:, :, None] - col_energy[None, None, :]
    return (ladder / denom).astype(jnp.bfloat16)
```

```python
import jax
import jax.numpy as jnp
from jax import lax
from jax.experimental import pallas as pl
from jax.experimental.pallas import tpu as pltpu
from jax.sharding import Mesh, PartitionSpec as P

NJ = 16
TILE = 128
NZ, NX, NC, NY = 12, 4, 2, 8
ROW = ("z", "x", "core")
CHUNKS = 4


def ladder_kernel(cols_ref, left_ref, tiles_hbm, out_ref, tiles_ref, where_ref, sems):
    kr, slots = cols_ref.shape
    per = kr // CHUNKS
    empty = kr * slots

    def chunk(c):
        span = pl.ds(c * per * slots, per * slots)
        return pltpu.make_async_copy(tiles_hbm.at[span], tiles_ref.at[span], sems.at[c])

    for c in range(CHUNKS):
        chunk(c).start()
    tiles_ref[empty] = jnp.zeros((TILE, TILE), jnp.bfloat16)

    def locate(k, carry):
        for j in range(NJ + 1):
            where_ref[k * (NJ + 1) + j] = empty
        for s in range(slots):
            where_ref[k * (NJ + 1) + cols_ref[k, s] + 1] = k * slots + s
        return carry

    lax.fori_loop(0, kr, locate, 0)

    def tile(k, j):
        return tiles_ref[where_ref[k * (NJ + 1) + j + 1]]

    def pair(k, j):
        return jnp.concatenate([tile(k, j), tile(k + 1, j)], axis=0)

    for c in range(CHUNKS):
        chunk(c).wait()
        for j in range(0, NJ, 2):
            span = pl.ds(j * TILE, 2 * TILE)
            acc = None if c == 0 else out_ref[:, span]
            for k in range(c * per, (c + 1) * per, 2):
                right = jnp.concatenate([pair(k, j), pair(k, j + 1)], axis=1)
                part = jnp.dot(
                    left_ref[:, pl.ds(k * TILE, 2 * TILE)], right,
                    preferred_element_type=jnp.float32,
                )
                acc = part if acc is None else acc + part
            out_ref[:, span] = acc


def ladder(left, integrals, tile_cols):
    kr, slots, _, _ = integrals.shape
    rows = left.shape[0]
    return pl.pallas_call(
        ladder_kernel,
        out_shape=jax.ShapeDtypeStruct((rows, NJ * TILE), jnp.float32),
        in_specs=[
            pl.BlockSpec(memory_space=pltpu.SMEM),
            pl.BlockSpec(memory_space=pltpu.VMEM),
            pl.BlockSpec(memory_space=pl.ANY),
        ],
        out_specs=pl.BlockSpec(memory_space=pltpu.VMEM),
        scratch_shapes=[
            pltpu.VMEM((kr * slots + 1, TILE, TILE), jnp.bfloat16),
            pltpu.SMEM((kr * (NJ + 1),), jnp.int32),
            pltpu.SemaphoreType.DMA((CHUNKS,)),
        ],
        compiler_params=pltpu.CompilerParams(vmem_limit_bytes=40 * 2**20),
    )(tile_cols, left, integrals.reshape(kr * slots, TILE, TILE))


def per_device(amplitudes, integrals, tile_cols, pair_energy, col_energy):
    blocks, pairs, depth = amplitudes.shape
    left = amplitudes.reshape(NZ, NX, NC, pairs, depth).transpose(2, 1, 0, 3, 4)
    left = left.reshape(blocks * pairs, depth)
    whole = ladder(left, integrals, tile_cols)
    half = blocks * pairs // NC
    core = lax.axis_index("core")
    mine = lax.dynamic_slice_in_dim(whole, core * half, half, 0)
    other = lax.dynamic_slice_in_dim(whole, (1 - core) * half, half, 0)
    other = lax.ppermute(other, "core", [(0, 1), (1, 0)])
    chip = (mine + other).reshape(NX, NZ * pairs, NJ * TILE)
    chip = lax.all_to_all(chip, "x", 0, 0, tiled=True)
    plane = jnp.sum(chip, axis=0)
    plane = plane.reshape(NZ, pairs, NY, NJ * TILE // NY).transpose(0, 2, 1, 3)
    plane = plane.reshape(NZ * NY, pairs, NJ * TILE // NY)
    owned = lax.all_to_all(plane, ("z", "y"), 0, 0, tiled=True)
    owned = jnp.sum(owned.reshape(NZ, NY * pairs, NJ * TILE // NY), axis=0, keepdims=True)
    denom = pair_energy[:, :, None] - col_energy[None, None, :]
    return (owned / denom).astype(jnp.bfloat16)


def solution(mesh):
    fine = Mesh(mesh.devices.reshape(NZ, NX, NC, NY), ("z", "x", "core", "y"))
    in_specs = (
        P(None, "y", ROW),
        P(ROW, None, None, None),
        P(ROW, None),
        P(ROW, None),
        P("y"),
    )
    out_specs = P(ROW, None, "y")
    return jax.shard_map(
        per_device, mesh=fine, in_specs=in_specs, out_specs=out_specs, check_vma=False
    )
```

```python
import jax
import jax.numpy as jnp
from jax import lax
from jax.experimental import pallas as pl
from jax.experimental.pallas import tpu as pltpu
from jax.sharding import Mesh, PartitionSpec as P

NJ = 16
TILE = 128
NZ, NX, NC, NY = 12, 4, 2, 8
ROW = ("z", "x", "core")
CHUNKS = 4
AHEAD = 2
LIMIT = 52 * 2**20


def ladder_kernel(core_ref, cols_hbm, left_hbm, tiles_hbm, send_ref, keep_ref,
                  cols_ref, left_ref, tiles_ref, where_ref, cols_sem, left_sems, tile_sems):
    slots, kr = cols_ref.shape
    half, width = send_ref.shape
    per = kr // CHUNKS
    empty = kr * slots
    stride = NJ + 1
    core = core_ref[0]

    def copies(c):
        depth = pl.ds(c * per * TILE, per * TILE)
        span = pl.ds(c * per * slots, per * slots)
        return (
            pltpu.make_async_copy(left_hbm.at[..., depth], left_ref.at[..., depth], left_sems.at[c]),
            pltpu.make_async_copy(tiles_hbm.at[span], tiles_ref.at[span], tile_sems.at[c]),
        )

    def start(c):
        for copy in copies(c):
            copy.start()

    fetch = pltpu.make_async_copy(cols_hbm, cols_ref, cols_sem)
    fetch.start()
    for c in range(AHEAD):
        start(c)
    tiles_ref[empty] = jnp.zeros((TILE, TILE), jnp.bfloat16)
    for at in range(kr * stride):
        where_ref[at] = empty
    fetch.wait()
    for k in range(kr):
        found = [cols_ref[s, k] for s in range(slots)]
        for s in range(slots):
            where_ref[k * stride + found[s] + 1] = k * slots + s

    def column(first, j):
        return jnp.concatenate(
            [tiles_ref[where_ref[(first + i) * stride + j + 1]] for i in range(per)], axis=0
        )

    for c in range(CHUNKS):
        for copy in copies(c):
            copy.wait()
        if c + AHEAD < CHUNKS:
            start(c + AHEAD)
        first = c * per
        depth = pl.ds(first * TILE, per * TILE)
        left = jnp.concatenate(
            [left_ref[:, x, side, :, depth] for side in (1 - core, core) for x in range(NX)],
            axis=0,
        ).reshape(2 * half, per * TILE)
        for j in range(0, NJ, 2):
            span = pl.ds(j * TILE, 2 * TILE)
            right = jnp.concatenate([column(first, j), column(first, j + 1)], axis=1)
            part = jnp.dot(left, right, preferred_element_type=jnp.float32)
            if c == 0:
                send_ref[:, span] = part[:half]
                keep_ref[:, span] = part[half:]
            else:
                send_ref[:, span] += part[:half]
                keep_ref[:, span] += part[half:]


def ladder(core, left, integrals, tile_cols):
    kr, slots, _, _ = integrals.shape
    blocks, pairs, depth = left.shape
    left = left.reshape(NZ, NX, NC, pairs, depth)
    half = jax.ShapeDtypeStruct((blocks * pairs // NC, NJ * TILE), jnp.float32)
    return pl.pallas_call(
        ladder_kernel,
        out_shape=(half, half),
        in_specs=[
            pl.BlockSpec(memory_space=pltpu.SMEM),
            pl.BlockSpec(memory_space=pl.ANY),
            pl.BlockSpec(memory_space=pl.ANY),
            pl.BlockSpec(memory_space=pl.ANY),
        ],
        out_specs=(pl.BlockSpec(memory_space=pltpu.VMEM), pl.BlockSpec(memory_space=pltpu.VMEM)),
        scratch_shapes=[
            pltpu.SMEM((slots, kr), jnp.int32),
            pltpu.VMEM(left.shape, jnp.bfloat16),
            pltpu.VMEM((kr * slots + 1, TILE, TILE), jnp.bfloat16),
            pltpu.SMEM((kr * (NJ + 1),), jnp.int32),
            pltpu.SemaphoreType.DMA(()),
            pltpu.SemaphoreType.DMA((CHUNKS,)),
            pltpu.SemaphoreType.DMA((CHUNKS,)),
        ],
        compiler_params=pltpu.CompilerParams(vmem_limit_bytes=LIMIT),
    )(core.reshape(1), tile_cols.T, left, integrals.reshape(kr * slots, TILE, TILE))


def per_device(amplitudes, integrals, tile_cols, pair_energy, col_energy):
    pairs = amplitudes.shape[1]
    core = lax.axis_index("core")
    send, keep = ladder(core, amplitudes, integrals, tile_cols)
    other = lax.ppermute(send, "core", [(0, 1), (1, 0)])
    chip = (keep + other).reshape(NX, NZ * pairs, NJ * TILE)
    chip = lax.all_to_all(chip, "x", 0, 0, tiled=True)
    plane = jnp.sum(chip, axis=0)
    plane = plane.reshape(NZ, pairs, NY, NJ * TILE // NY).transpose(0, 2, 1, 3)
    plane = plane.reshape(NZ * NY, pairs, NJ * TILE // NY)
    owned = lax.all_to_all(plane, ("z", "y"), 0, 0, tiled=True)
    owned = jnp.sum(owned.reshape(NZ, NY * pairs, NJ * TILE // NY), axis=0, keepdims=True)
    denom = pair_energy[:, :, None] - col_energy[None, None, :]
    return (owned / denom).astype(jnp.bfloat16)


def solution(mesh):
    fine = Mesh(mesh.devices.reshape(NZ, NX, NC, NY), ("z", "x", "core", "y"))
    in_specs = (
        P(None, "y", ROW),
        P(ROW, None, None, None),
        P(ROW, None),
        P(ROW, None),
        P("y"),
    )
    out_specs = P(ROW, None, "y")
    return jax.shard_map(
        per_device, mesh=fine, in_specs=in_specs, out_specs=out_specs, check_vma=False
    )
```

```python
import jax
import jax.numpy as jnp
from jax import lax
from jax.experimental import pallas as pl
from jax.experimental.pallas import tpu as pltpu
from jax.sharding import Mesh, PartitionSpec as P

NJ = 16
TILE = 128
NH, NL, NX, NC, NY = 6, 2, 4, 2, 8
FOLD = 2
ROW = ("zh", "zl", "x", "core")
CHUNKS = 4
AHEAD = 2
LIMIT = 52 * 2**20


def ladder_kernel(core_ref, cols_hbm, left_hbm, tiles_hbm, send_ref, keep_ref,
                  cols_ref, left_ref, tiles_ref, where_ref, acc_ref, cols_sem, left_sems, tile_sems):
    slots, kr = cols_ref.shape
    groups, rows, width = send_ref.shape
    rows //= FOLD
    half = groups * rows
    per = kr // CHUNKS
    empty = kr * slots
    stride = NJ + 1
    core = core_ref[0]

    def copies(c):
        depth = pl.ds(c * per * TILE, per * TILE)
        span = pl.ds(c * per * slots, per * slots)
        return (
            pltpu.make_async_copy(left_hbm.at[..., depth], left_ref.at[..., depth], left_sems.at[c]),
            pltpu.make_async_copy(tiles_hbm.at[span], tiles_ref.at[span], tile_sems.at[c]),
        )

    def start(c):
        for copy in copies(c):
            copy.start()

    fetch = pltpu.make_async_copy(cols_hbm, cols_ref, cols_sem)
    fetch.start()
    for c in range(AHEAD):
        start(c)
    tiles_ref[empty] = jnp.zeros((TILE, TILE), jnp.bfloat16)
    for at in range(kr * stride):
        where_ref[at] = empty
    fetch.wait()
    for k in range(kr):
        found = [cols_ref[s, k] for s in range(slots)]
        for s in range(slots):
            where_ref[k * stride + found[s] + 1] = k * slots + s

    def column(first, j):
        return jnp.concatenate(
            [tiles_ref[where_ref[(first + i) * stride + j + 1]] for i in range(per)], axis=0
        )

    for c in range(CHUNKS):
        for copy in copies(c):
            copy.wait()
        if c + AHEAD < CHUNKS:
            start(c + AHEAD)
        first = c * per
        depth = pl.ds(first * TILE, per * TILE)
        left = jnp.concatenate(
            [left_ref[:, zl, x, side, :, depth]
             for side in (1 - core, core) for x in range(NX) for zl in range(NL)],
            axis=0,
        ).reshape(2 * half, per * TILE)
        for j in range(0, NJ, 2):
            span = pl.ds(j * TILE, 2 * TILE)
            right = jnp.concatenate([column(first, j), column(first, j + 1)], axis=1)
            part = jnp.dot(left, right, preferred_element_type=jnp.float32)
            if c > 0:
                part += acc_ref[:, span]
            if c < CHUNKS - 1:
                acc_ref[:, span] = part
                continue
            at = pl.ds(j * TILE // width * rows, rows)
            lanes = pl.ds(j * TILE % width, 2 * TILE)
            for g in range(groups):
                send_ref[g, at, lanes] = part[g * rows:(g + 1) * rows]
                keep_ref[g, at, lanes] = part[half + g * rows:half + (g + 1) * rows]


def ladder(core, left, integrals, tile_cols):
    kr, slots, _, _ = integrals.shape
    blocks, pairs, depth = left.shape
    left = left.reshape(NH, NL, NX, NC, pairs, depth)
    half = jax.ShapeDtypeStruct((NX * NL, FOLD * NH * pairs, NJ * TILE // FOLD), jnp.float32)
    return pl.pallas_call(
        ladder_kernel,
        out_shape=(half, half),
        in_specs=[
            pl.BlockSpec(memory_space=pltpu.SMEM),
            pl.BlockSpec(memory_space=pl.ANY),
            pl.BlockSpec(memory_space=pl.ANY),
            pl.BlockSpec(memory_space=pl.ANY),
        ],
        out_specs=(pl.BlockSpec(memory_space=pltpu.VMEM), pl.BlockSpec(memory_space=pltpu.VMEM)),
        scratch_shapes=[
            pltpu.SMEM((slots, kr), jnp.int32),
            pltpu.VMEM(left.shape, jnp.bfloat16),
            pltpu.VMEM((kr * slots + 1, TILE, TILE), jnp.bfloat16),
            pltpu.SMEM((kr * (NJ + 1),), jnp.int32),
            pltpu.VMEM((blocks * pairs, NJ * TILE), jnp.float32),
            pltpu.SemaphoreType.DMA(()),
            pltpu.SemaphoreType.DMA((CHUNKS,)),
            pltpu.SemaphoreType.DMA((CHUNKS,)),
        ],
        compiler_params=pltpu.CompilerParams(vmem_limit_bytes=LIMIT),
    )(core.reshape(1), tile_cols.T, left, integrals.reshape(kr * slots, TILE, TILE))


def per_device(amplitudes, integrals, tile_cols, pair_energy, col_energy):
    pairs = amplitudes.shape[1]
    core = lax.axis_index("core")
    send, keep = ladder(core, amplitudes, integrals, tile_cols)
    other = lax.ppermute(send, "core", [(0, 1), (1, 0)])
    chip = lax.all_to_all(keep + other, ("x", "zl"), 0, 0, tiled=True)
    width = NJ * TILE // NY
    plane = jnp.sum(chip, axis=0).reshape(FOLD, NH, pairs, NY // FOLD, width)
    plane = plane.transpose(1, 0, 3, 2, 4).reshape(NH * NY, pairs, width)
    owned = lax.all_to_all(plane, ("zh", "y"), 0, 0, tiled=True)
    owned = jnp.sum(owned.reshape(NH, NY * pairs, width), axis=0, keepdims=True)
    denom = pair_energy[:, :, None] - col_energy[None, None, :]
    return (owned / denom).astype(jnp.bfloat16)


def solution(mesh):
    fine = Mesh(mesh.devices.reshape(NH, NL, NX, NC, NY), ("zh", "zl", "x", "core", "y"))
    in_specs = (
        P(None, "y", ROW),
        P(ROW, None, None, None),
        P(ROW, None),
        P(ROW, None),
        P("y"),
    )
    out_specs = P(ROW, None, "y")
    return jax.shard_map(
        per_device, mesh=fine, in_specs=in_specs, out_specs=out_specs, check_vma=False
    )
```

```python
import jax
import jax.numpy as jnp
from jax import lax
from jax.experimental import pallas as pl
from jax.experimental.pallas import tpu as pltpu
from jax.sharding import Mesh, PartitionSpec as P

NJ = 16
TILE = 128
NH, NL, NX, NC, NY = 6, 2, 4, 2, 8
FOLD = 2
ROW = ("zh", "zl", "x", "core")
BOUNDS = (0, 4, 8, 14, 20, 26, 32)
CHUNKS = len(BOUNDS) - 1
AHEAD = 3
LIMIT = 32 * 2**20


def ladder_kernel(core_ref, cols_hbm, left_hbm, tiles_hbm, send_ref, keep_ref,
                  cols_ref, left_ref, tiles_ref, where_ref, acc_ref, cols_sem, left_sems, tile_sems):
    slots, kr = cols_ref.shape
    groups, rows, width = send_ref.shape
    rows //= FOLD
    half = groups * rows
    empty = kr * slots
    stride = NJ + 1
    core = core_ref[0]

    def copies(c):
        first, per = BOUNDS[c], BOUNDS[c + 1] - BOUNDS[c]
        depth = pl.ds(first * TILE, per * TILE)
        span = pl.ds(first * slots, per * slots)
        return (
            pltpu.make_async_copy(left_hbm.at[..., depth], left_ref.at[..., depth], left_sems.at[c]),
            pltpu.make_async_copy(tiles_hbm.at[span], tiles_ref.at[span], tile_sems.at[c]),
        )

    def start(c):
        for copy in copies(c):
            copy.start()

    fetch = pltpu.make_async_copy(cols_hbm, cols_ref, cols_sem)
    fetch.start()
    for c in range(AHEAD):
        start(c)
    tiles_ref[empty] = jnp.zeros((TILE, TILE), jnp.bfloat16)
    for at in range(kr * stride):
        where_ref[at] = empty
    fetch.wait()
    for k in range(kr):
        found = [cols_ref[s, k] for s in range(slots)]
        for s in range(slots):
            where_ref[k * stride + found[s] + 1] = k * slots + s

    def column(first, per, j):
        return jnp.concatenate(
            [tiles_ref[where_ref[(first + i) * stride + j + 1]] for i in range(per)], axis=0
        )

    for c in range(CHUNKS):
        for copy in copies(c):
            copy.wait()
        if c + AHEAD < CHUNKS:
            start(c + AHEAD)
        first, per = BOUNDS[c], BOUNDS[c + 1] - BOUNDS[c]
        depth = pl.ds(first * TILE, per * TILE)
        left = jnp.concatenate(
            [left_ref[:, zl, x, side, :, depth]
             for side in (1 - core, core) for x in range(NX) for zl in range(NL)],
            axis=0,
        ).reshape(2 * half, per * TILE)
        for j in range(0, NJ, 2):
            span = pl.ds(j * TILE, 2 * TILE)
            right = jnp.concatenate([column(first, per, j), column(first, per, j + 1)], axis=1)
            part = jnp.dot(left, right, preferred_element_type=jnp.float32)
            if c > 0:
                part += acc_ref[:, span]
            if c < CHUNKS - 1:
                acc_ref[:, span] = part
                continue
            at = pl.ds(j * TILE // width * rows, rows)
            lanes = pl.ds(j * TILE % width, 2 * TILE)
            for g in range(groups):
                send_ref[g, at, lanes] = part[g * rows:(g + 1) * rows]
                keep_ref[g, at, lanes] = part[half + g * rows:half + (g + 1) * rows]


def ladder(core, left, integrals, tile_cols):
    kr, slots, _, _ = integrals.shape
    blocks, pairs, depth = left.shape
    left = left.reshape(NH, NL, NX, NC, pairs, depth)
    half = jax.ShapeDtypeStruct((NX * NL, FOLD * NH * pairs, NJ * TILE // FOLD), jnp.float32)
    return pl.pallas_call(
        ladder_kernel,
        out_shape=(half, half),
        in_specs=[
            pl.BlockSpec(memory_space=pltpu.SMEM),
            pl.BlockSpec(memory_space=pl.ANY),
            pl.BlockSpec(memory_space=pl.ANY),
            pl.BlockSpec(memory_space=pl.ANY),
        ],
        out_specs=(pl.BlockSpec(memory_space=pltpu.VMEM), pl.BlockSpec(memory_space=pltpu.VMEM)),
        scratch_shapes=[
            pltpu.SMEM((slots, kr), jnp.int32),
            pltpu.VMEM(left.shape, jnp.bfloat16),
            pltpu.VMEM((kr * slots + 1, TILE, TILE), jnp.bfloat16),
            pltpu.SMEM((kr * (NJ + 1),), jnp.int32),
            pltpu.VMEM((blocks * pairs, NJ * TILE), jnp.float32),
            pltpu.SemaphoreType.DMA(()),
            pltpu.SemaphoreType.DMA((CHUNKS,)),
            pltpu.SemaphoreType.DMA((CHUNKS,)),
        ],
        compiler_params=pltpu.CompilerParams(vmem_limit_bytes=LIMIT),
    )(
        core.reshape(1),
        pltpu.with_memory_space_constraint(tile_cols.T, pltpu.HBM),
        pltpu.with_memory_space_constraint(left, pltpu.HBM),
        pltpu.with_memory_space_constraint(integrals.reshape(kr * slots, TILE, TILE), pltpu.HBM),
    )


def per_device(amplitudes, integrals, tile_cols, pair_energy, col_energy):
    pairs = amplitudes.shape[1]
    core = lax.axis_index("core")
    send, keep = ladder(core, amplitudes, integrals, tile_cols)
    other = lax.ppermute(send, "core", [(0, 1), (1, 0)])
    chip = lax.all_to_all(keep + other, ("x", "zl"), 0, 0, tiled=True)
    width = NJ * TILE // NY
    plane = jnp.sum(chip, axis=0).reshape(FOLD, NH, pairs, NY // FOLD, width)
    plane = plane.transpose(1, 0, 3, 2, 4).reshape(NH * NY, pairs, width)
    owned = lax.all_to_all(plane, ("zh", "y"), 0, 0, tiled=True)
    owned = jnp.sum(owned.reshape(NH, NY * pairs, width), axis=0, keepdims=True)
    denom = pair_energy[:, :, None] - col_energy[None, None, :]
    return (owned / denom).astype(jnp.bfloat16)


def solution(mesh):
    fine = Mesh(mesh.devices.reshape(NH, NL, NX, NC, NY), ("zh", "zl", "x", "core", "y"))
    in_specs = (
        P(None, "y", ROW),
        P(ROW, None, None, None),
        P(ROW, None),
        P(ROW, None),
        P("y"),
    )
    out_specs = P(ROW, None, "y")
    return jax.shard_map(
        per_device, mesh=fine, in_specs=in_specs, out_specs=out_specs, check_vma=False
    )
```

```python
import jax
import jax.numpy as jnp
from jax import lax
from jax.experimental import pallas as pl
from jax.experimental.pallas import tpu as pltpu
from jax.sharding import Mesh, PartitionSpec as P

NJ = 16
TILE = 128
NH, NL, NX, NC, NY = 6, 2, 4, 2, 8
FOLD = 2
Z_ORDER = tuple((i + NH // 2) % NH for i in range(NH))
Y_ORDER = tuple((i + NY // 2) % NY for i in range(NY))
X_ORDER = (2, 3, 0, 1)
L_ORDER = (1, 0)
PLANE = [x * NL + zl for x in X_ORDER for zl in L_ORDER]
COLUMN = [zh * NY + y for zh in Z_ORDER for y in Y_ORDER]
ROW = ("zh", "zl", "x", "core")
BOUNDS = (0, 4, 8, 14, 20, 26, 32)
CHUNKS = len(BOUNDS) - 1
AHEAD = 3
LIMIT = 32 * 2**20


def ladder_kernel(core_ref, cols_hbm, left_hbm, tiles_hbm, send_ref, keep_ref,
                  cols_ref, left_ref, tiles_ref, where_ref, acc_ref, cols_sem, left_sems, tile_sems):
    slots, kr = cols_ref.shape
    groups, rows, width = send_ref.shape
    rows //= FOLD
    half = groups * rows
    empty = kr * slots
    stride = NJ + 1
    core = core_ref[0]

    def copies(c):
        first, per = BOUNDS[c], BOUNDS[c + 1] - BOUNDS[c]
        depth = pl.ds(first * TILE, per * TILE)
        span = pl.ds(first * slots, per * slots)
        return (
            pltpu.make_async_copy(left_hbm.at[..., depth], left_ref.at[..., depth], left_sems.at[c]),
            pltpu.make_async_copy(tiles_hbm.at[span], tiles_ref.at[span], tile_sems.at[c]),
        )

    def start(c):
        for copy in copies(c):
            copy.start()

    fetch = pltpu.make_async_copy(cols_hbm, cols_ref, cols_sem)
    fetch.start()
    for c in range(AHEAD):
        start(c)
    tiles_ref[empty] = jnp.zeros((TILE, TILE), jnp.bfloat16)
    for at in range(kr * stride):
        where_ref[at] = empty
    fetch.wait()
    for k in range(kr):
        found = [cols_ref[s, k] for s in range(slots)]
        for s in range(slots):
            where_ref[k * stride + found[s] + 1] = k * slots + s

    def column(first, per, j):
        return jnp.concatenate(
            [tiles_ref[where_ref[(first + i) * stride + j + 1]] for i in range(per)], axis=0
        )

    for c in range(CHUNKS):
        for copy in copies(c):
            copy.wait()
        if c + AHEAD < CHUNKS:
            start(c + AHEAD)
        first, per = BOUNDS[c], BOUNDS[c + 1] - BOUNDS[c]
        depth = pl.ds(first * TILE, per * TILE)
        left = jnp.concatenate(
            [left_ref[pl.ds(zh, NH // 2), zl, x, side, :, depth]
             for side in (1 - core, core) for x in X_ORDER for zl in L_ORDER
             for zh in (NH // 2, 0)],
            axis=0,
        ).reshape(2 * half, per * TILE)
        for j in range(0, NJ, 2):
            span = pl.ds(j * TILE, 2 * TILE)
            right = jnp.concatenate([column(first, per, j), column(first, per, j + 1)], axis=1)
            part = jnp.dot(left, right, preferred_element_type=jnp.float32)
            if c > 0:
                part += acc_ref[:, span]
            if c < CHUNKS - 1:
                acc_ref[:, span] = part
                continue
            at = pl.ds((1 - j * TILE // width) * rows, rows)
            lanes = pl.ds(j * TILE % width, 2 * TILE)
            for g in range(groups):
                send_ref[g, at, lanes] = part[g * rows:(g + 1) * rows]
                keep_ref[g, at, lanes] = part[half + g * rows:half + (g + 1) * rows]


def ladder(core, left, integrals, tile_cols):
    kr, slots, _, _ = integrals.shape
    blocks, pairs, depth = left.shape
    left = left.reshape(NH, NL, NX, NC, pairs, depth)
    half = jax.ShapeDtypeStruct((NX * NL, FOLD * NH * pairs, NJ * TILE // FOLD), jnp.float32)
    return pl.pallas_call(
        ladder_kernel,
        out_shape=(half, half),
        in_specs=[
            pl.BlockSpec(memory_space=pltpu.SMEM),
            pl.BlockSpec(memory_space=pl.ANY),
            pl.BlockSpec(memory_space=pl.ANY),
            pl.BlockSpec(memory_space=pl.ANY),
        ],
        out_specs=(pl.BlockSpec(memory_space=pltpu.VMEM), pl.BlockSpec(memory_space=pltpu.VMEM)),
        scratch_shapes=[
            pltpu.SMEM((slots, kr), jnp.int32),
            pltpu.VMEM(left.shape, jnp.bfloat16),
            pltpu.VMEM((kr * slots + 1, TILE, TILE), jnp.bfloat16),
            pltpu.SMEM((kr * (NJ + 1),), jnp.int32),
            pltpu.VMEM((blocks * pairs, NJ * TILE), jnp.float32),
            pltpu.SemaphoreType.DMA(()),
            pltpu.SemaphoreType.DMA((CHUNKS,)),
            pltpu.SemaphoreType.DMA((CHUNKS,)),
        ],
        compiler_params=pltpu.CompilerParams(vmem_limit_bytes=LIMIT),
    )(
        core.reshape(1),
        pltpu.with_memory_space_constraint(tile_cols.T, pltpu.HBM),
        pltpu.with_memory_space_constraint(left, pltpu.HBM),
        pltpu.with_memory_space_constraint(integrals.reshape(kr * slots, TILE, TILE), pltpu.HBM),
    )


def per_device(amplitudes, integrals, tile_cols, pair_energy, col_energy):
    pairs = amplitudes.shape[1]
    core = lax.axis_index("core")
    send, keep = ladder(core, amplitudes, integrals, tile_cols)
    other = lax.ppermute(send, "core", [(0, 1), (1, 0)])
    chip = lax.all_to_all(keep + other, ("x", "zl"), 0, 0, tiled=True, axis_index_groups=[PLANE])
    width = NJ * TILE // NY
    plane = jnp.sum(chip, axis=0).reshape(FOLD, NH, pairs, NY // FOLD, width)
    plane = plane.transpose(1, 0, 3, 2, 4).reshape(NH * NY, pairs, width)
    owned = lax.all_to_all(plane, ("zh", "y"), 0, 0, tiled=True, axis_index_groups=[COLUMN])
    owned = jnp.sum(owned.reshape(NH, NY * pairs, width), axis=0, keepdims=True)
    owned = jnp.roll(owned, NY // 2 * pairs, axis=1)
    denom = pair_energy[:, :, None] - col_energy[None, None, :]
    return (owned / denom).astype(jnp.bfloat16)


def solution(mesh):
    fine = Mesh(mesh.devices.reshape(NH, NL, NX, NC, NY), ("zh", "zl", "x", "core", "y"))
    in_specs = (
        P(None, "y", ROW),
        P(ROW, None, None, None),
        P(ROW, None),
        P(ROW, None),
        P("y"),
    )
    out_specs = P(ROW, None, "y")
    return jax.shard_map(
        per_device, mesh=fine, in_specs=in_specs, out_specs=out_specs, check_vma=False
    )
```

```python
import jax
import jax.numpy as jnp
from jax import lax
from jax.experimental import pallas as pl
from jax.experimental.pallas import tpu as pltpu
from jax.sharding import Mesh, PartitionSpec as P

NJ = 16
TILE = 128
NH, NL, NX, NC, NY = 6, 2, 4, 2, 8
FOLD = 2
Z_ORDER = tuple((i + 4) % NH for i in range(NH))
Y_ORDER = tuple((i + NY // 2) % NY for i in range(NY))
X_ORDER = (2, 3, 0, 1)
L_ORDER = (1, 0)
PLANE = [x * NL + zl for x in X_ORDER for zl in L_ORDER]
COLUMN = [zh * NY + y for zh in Z_ORDER for y in Y_ORDER]
ROW = ("zh", "zl", "x", "core")
BOUNDS = (0, 4, 8, 14, 20, 26, 32)
CHUNKS = len(BOUNDS) - 1
AHEAD = 3
LIMIT = 32 * 2**20


def ladder_kernel(core_ref, cols_hbm, left_hbm, tiles_hbm, send_ref, keep_ref,
                  cols_ref, left_ref, tiles_ref, where_ref, acc_ref, cols_sem, left_sems, tile_sems):
    slots, kr = cols_ref.shape
    groups, rows, width = send_ref.shape
    rows //= FOLD
    half = groups * rows
    empty = kr * slots
    stride = NJ + 1
    core = core_ref[0]

    def copies(c):
        first, per = BOUNDS[c], BOUNDS[c + 1] - BOUNDS[c]
        depth = pl.ds(first * TILE, per * TILE)
        span = pl.ds(first * slots, per * slots)
        return (
            pltpu.make_async_copy(left_hbm.at[..., depth], left_ref.at[..., depth], left_sems.at[c]),
            pltpu.make_async_copy(tiles_hbm.at[span], tiles_ref.at[span], tile_sems.at[c]),
        )

    def start(c):
        for copy in copies(c):
            copy.start()

    fetch = pltpu.make_async_copy(cols_hbm, cols_ref, cols_sem)
    fetch.start()
    for c in range(AHEAD):
        start(c)
    tiles_ref[empty] = jnp.zeros((TILE, TILE), jnp.bfloat16)
    for at in range(kr * stride):
        where_ref[at] = empty
    fetch.wait()
    for k in range(kr):
        found = [cols_ref[s, k] for s in range(slots)]
        for s in range(slots):
            where_ref[k * stride + found[s] + 1] = k * slots + s

    def column(first, per, j):
        return jnp.concatenate(
            [tiles_ref[where_ref[(first + i) * stride + j + 1]] for i in range(per)], axis=0
        )

    for c in range(CHUNKS):
        for copy in copies(c):
            copy.wait()
        if c + AHEAD < CHUNKS:
            start(c + AHEAD)
        first, per = BOUNDS[c], BOUNDS[c + 1] - BOUNDS[c]
        depth = pl.ds(first * TILE, per * TILE)
        left = jnp.concatenate(
            [left_ref[zh, zl, x, side, :, depth]
             for side in (1 - core, core) for x in X_ORDER for zl in L_ORDER
             for zh in (pl.ds(4, NH - 4), pl.ds(0, 4))],
            axis=0,
        ).reshape(2 * half, per * TILE)
        for j in range(0, NJ, 2):
            span = pl.ds(j * TILE, 2 * TILE)
            right = jnp.concatenate([column(first, per, j), column(first, per, j + 1)], axis=1)
            part = jnp.dot(left, right, preferred_element_type=jnp.float32)
            if c > 0:
                part += acc_ref[:, span]
            if c < CHUNKS - 1:
                acc_ref[:, span] = part
                continue
            at = pl.ds((1 - j * TILE // width) * rows, rows)
            lanes = pl.ds(j * TILE % width, 2 * TILE)
            for g in range(groups):
                send_ref[g, at, lanes] = part[g * rows:(g + 1) * rows]
                keep_ref[g, at, lanes] = part[half + g * rows:half + (g + 1) * rows]


def ladder(core, left, integrals, tile_cols):
    kr, slots, _, _ = integrals.shape
    blocks, pairs, depth = left.shape
    left = left.reshape(NH, NL, NX, NC, pairs, depth)
    half = jax.ShapeDtypeStruct((NX * NL, FOLD * NH * pairs, NJ * TILE // FOLD), jnp.float32)
    return pl.pallas_call(
        ladder_kernel,
        out_shape=(half, half),
        in_specs=[
            pl.BlockSpec(memory_space=pltpu.SMEM),
            pl.BlockSpec(memory_space=pl.ANY),
            pl.BlockSpec(memory_space=pl.ANY),
            pl.BlockSpec(memory_space=pl.ANY),
        ],
        out_specs=(pl.BlockSpec(memory_space=pltpu.VMEM), pl.BlockSpec(memory_space=pltpu.VMEM)),
        scratch_shapes=[
            pltpu.SMEM((slots, kr), jnp.int32),
            pltpu.VMEM(left.shape, jnp.bfloat16),
            pltpu.VMEM((kr * slots + 1, TILE, TILE), jnp.bfloat16),
            pltpu.SMEM((kr * (NJ + 1),), jnp.int32),
            pltpu.VMEM((blocks * pairs, NJ * TILE), jnp.float32),
            pltpu.SemaphoreType.DMA(()),
            pltpu.SemaphoreType.DMA((CHUNKS,)),
            pltpu.SemaphoreType.DMA((CHUNKS,)),
        ],
        compiler_params=pltpu.CompilerParams(vmem_limit_bytes=LIMIT),
    )(
        core.reshape(1),
        pltpu.with_memory_space_constraint(tile_cols.T, pltpu.HBM),
        pltpu.with_memory_space_constraint(left, pltpu.HBM),
        pltpu.with_memory_space_constraint(integrals.reshape(kr * slots, TILE, TILE), pltpu.HBM),
    )


def per_device(amplitudes, integrals, tile_cols, pair_energy, col_energy):
    pairs = amplitudes.shape[1]
    core = lax.axis_index("core")
    send, keep = ladder(core, amplitudes, integrals, tile_cols)
    other = lax.ppermute(send, "core", [(0, 1), (1, 0)])
    chip = lax.all_to_all(keep + other, ("x", "zl"), 0, 0, tiled=True, axis_index_groups=[PLANE])
    width = NJ * TILE // NY
    plane = jnp.sum(chip, axis=0).reshape(FOLD, NH, pairs, NY // FOLD, width)
    plane = plane.transpose(1, 0, 3, 2, 4).reshape(NH * NY, pairs, width)
    owned = lax.all_to_all(plane, ("zh", "y"), 0, 0, tiled=True, axis_index_groups=[COLUMN])
    owned = jnp.sum(owned.reshape(NH, NY * pairs, width), axis=0, keepdims=True)
    owned = jnp.roll(owned, NY // 2 * pairs, axis=1)
    denom = pair_energy[:, :, None] - col_energy[None, None, :]
    return (owned / denom).astype(jnp.bfloat16)


def solution(mesh):
    fine = Mesh(mesh.devices.reshape(NH, NL, NX, NC, NY), ("zh", "zl", "x", "core", "y"))
    in_specs = (
        P(None, "y", ROW),
        P(ROW, None, None, None),
        P(ROW, None),
        P(ROW, None),
        P("y"),
    )
    out_specs = P(ROW, None, "y")
    return jax.shard_map(
        per_device, mesh=fine, in_specs=in_specs, out_specs=out_specs, check_vma=False
    )
```
